512 devices in a mesh: chan: 64 (over x, y, z_lo), sp: 8 (over z_hi, core).
Axes of the slice: x: 4, y: 8, z: 8 (z_hi: 4, z_lo: 2; z = z_hi * 2 + z_lo), core: 2. Of those that a mesh axis runs over, the one named last changes fastest.
Arguments:
- activations: bfloat16 [16, 64, 64, 256], P('sp', 'chan'), may hold values from -16 to 16
- weights: bfloat16 [27, 256, 256], replicated, may hold values from -0.078125 to 0.078125
- grad_output: bfloat16 [16, 64, 64, 256], P('sp', 'chan'), may hold values from -6 to 6
Outputs:
- output: bfloat16 [16, 64, 64, 256], P('sp', 'chan')
- grad_input: bfloat16 [16, 64, 64, 256], P('sp', 'chan')
- grad_weights: float32 [27, 256, 256], P(None, 'chan')
The draws below stay inside these ranges and needn't reach their ends.
All inputs are finite; a program needn't handle non-finite values.
Results may differ from the reference program's by a relative error of at most 0.001.
Values may be sent and summed in bfloat16 or wider, within the bound.
A program may use at most 64 MiB of HBM per device.

```python
import jax
import jax.numpy as jnp

CIN = 256
COUT = 256
TAPS = 27
WIDTH = 64
DEPTH = 16
HEIGHT = 64


def spiked(array, rng, source, target, shards_of, factor):
    owner, partner = [(jnp.arange(array.shape[axis_at]) // (array.shape[axis_at] // shards_of)).reshape([-1 if axis == axis_at else 1 for axis in range(array.ndim)]) for axis_at in (source, target)]
    chosen = jax.random.permutation(rng, shards_of)[partner]
    strong = (owner == chosen) | (owner == (partner + shards_of // 2) % shards_of)
    return jnp.where(strong, factor * array, array)


def steps_of(key, shape, shards, smallest, top_value):
    loudness = 1.0
    for position, shards_of in shards:
        heights = jax.random.uniform(jax.random.fold_in(jax.random.fold_in(key, 6), position), (shards_of,), jnp.float32, smallest / len(shards), top_value / len(shards))
        loudness = loudness * jnp.repeat(jnp.exp(heights), shape[position] // shards_of).reshape((-1,) + (1,) * (len(shape) - 1 - position))
    return loudness


def gaussian(own_key, shape, spread, most, pieces=(), dtype=jnp.bfloat16):
    entries = spread * jax.random.normal(own_key, shape, jnp.float32)
    if pieces:
        entries = entries * steps_of(own_key, shape, pieces, -0.22, 0.18)
    return jnp.clip(entries, -most, most).astype(dtype)


def gaussian_with(rng, dims, width, most, pieces, heavy, kind=jnp.bfloat16):
    result = width * jax.random.normal(rng, dims, jnp.float32)
    if pieces:
        result = result * steps_of(rng, dims, pieces, -0.22, 0.18)
    return jnp.clip(spiked(result, jax.random.fold_in(rng, 3), *heavy), -most, most).astype(kind)


def setup_inputs(seed: int = 0) -> dict:
    key_of = jax.random.split(jax.random.key(seed), 4)
    activations = gaussian_with(key_of[0], (DEPTH, HEIGHT, WIDTH, CIN), 1.0, 16.0, ((0, 8), (1, 64)), (1, 3, 64, 4.0))
    weights = gaussian(key_of[1], (TAPS, CIN, COUT), (TAPS * CIN) ** -0.5, 0.078125)
    grad_output = gaussian(key_of[2], (DEPTH, HEIGHT, WIDTH, COUT), 1.0, 6.0, ((0, 8), (1, 64)))
    return {"activations": activations, "weights": weights, "grad_output": grad_output}


def reference(activations, weights, grad_output):
    cell_count = DEPTH * HEIGHT * WIDTH
    spacing = ((1, 1), (1, 1), (1, 1), (0, 0))
    padded = jnp.pad(activations, spacing)
    grad_pad = jnp.pad(grad_output, spacing)
    flat_grad = grad_output.reshape(cell_count, COUT)
    forward = jnp.zeros((cell_count, COUT), jnp.float32)
    backward = jnp.zeros((cell_count, CIN), jnp.float32)
    filter_terms = []
    for tap_index in range(27):
        plane_off = tap_index // 9
        row_off = (tap_index // 3) % 3
        col_off = tap_index % 3
        window = padded[plane_off:plane_off + DEPTH, row_off:row_off + HEIGHT, col_off:col_off + WIDTH].reshape(cell_count, CIN)
        forward = forward + jnp.dot(window, weights[tap_index], preferred_element_type=jnp.float32)
        grad_window = grad_pad[2 - plane_off:2 - plane_off + DEPTH, 2 - row_off:2 - row_off + HEIGHT, 2 - col_off:2 - col_off + WIDTH].reshape(cell_count, COUT)
        backward = backward + jnp.dot(grad_window, weights[tap_index].T, preferred_element_type=jnp.float32)
        filter_terms.append(jnp.dot(window.T, flat_grad, preferred_element_type=jnp.float32))
    grad_weights = jnp.stack(filter_terms) * (float(cell_count) ** -0.5)
    output = forward.reshape(DEPTH, HEIGHT, WIDTH, COUT).astype(jnp.bfloat16)
    grad_input = backward.reshape(DEPTH, HEIGHT, WIDTH, CIN).astype(jnp.bfloat16)
    return output, grad_input, grad_weights
```

```python
import functools

import jax
import jax.numpy as jnp
from jax import lax
from jax.experimental import pallas as pl
from jax.experimental.pallas import tpu as pltpu
from jax.sharding import PartitionSpec as P

MESH = pl.DeviceIdType.MESH
F32 = jnp.float32
BF16 = jnp.bfloat16

LINES = 32
DEPTHS = 8


def shifted(value, by):
    width = value.shape[-2]
    rolled = pltpu.roll(value, by % width, value.ndim - 2)
    place = lax.broadcasted_iota(jnp.int32, value.shape, value.ndim - 2)
    return jnp.where(place == (0 if by == 1 else width - 1), 0.0, rolled)


def kernel(
    act_hbm, w_hbm, grad_hbm, out_ref, gin_ref, gw_ref,
    act_halo, grad_halo, w_v, act_t, act_all, grads, lhs, rhs, product, message, arrived, piece, pieces, mixed, total,
    in_sem, act_send, act_recv, g_send, g_recv, b_send, b_recv, c_send, c_recv, halo_send, halo_recv,
):
    q, s = lax.axis_index("chan"), lax.axis_index("sp")
    m, l = q // 2, q % 2
    h, c = s // 2, s % 2

    def at(line, side, depth):
        return (line * 2 + side, depth)

    barrier = pltpu.get_barrier_semaphore()

    def greet(device):
        pl.semaphore_signal(barrier, inc=1, device_id=device, device_id_type=MESH)

    n = l * 8 + s

    def greet_line(k, carry):
        peer = (n + k) % 16
        greet(at(m, peer // 8, peer % 8))
        return carry

    lax.fori_loop(1, 16, greet_line, 0)

    @pl.when(m > 0)
    def _():
        lax.fori_loop(0, DEPTHS, lambda k, t: (greet(at(m - 1, 1, k)), t)[1], 0)

    @pl.when(m < LINES - 1)
    def _():
        lax.fori_loop(0, DEPTHS, lambda k, t: (greet(at(m + 1, 0, k)), t)[1], 0)

    def greet_plane(k, carry):
        greet(at((m + k) % LINES, l, s))
        return carry

    lax.fori_loop(1, LINES, greet_plane, 0)

    own_grad = pltpu.make_async_copy(grad_hbm.at[:, 0], grad_halo.at[pl.ds(1, 2), 1], in_sem.at[0])
    own_act = pltpu.make_async_copy(act_hbm.at[:, 0], act_halo.at[pl.ds(1, 2), 1], in_sem.at[1])
    own_w = pltpu.make_async_copy(w_hbm, w_v, in_sem.at[2])
    own_grad.start()
    own_act.start()
    own_w.start()

    for halo in (act_halo, grad_halo):
        @pl.when(q == 0)
        def _(halo=halo):
            halo[:, 0] = jnp.zeros((4, 64, 256), BF16)

        @pl.when(q == 2 * LINES - 1)
        def _(halo=halo):
            halo[:, 2] = jnp.zeros((4, 64, 256), BF16)

        @pl.when(s == 0)
        def _(halo=halo):
            halo[0] = jnp.zeros((3, 64, 256), BF16)

        @pl.when(s == DEPTHS - 1)
        def _(halo=halo):
            halo[3] = jnp.zeros((3, 64, 256), BF16)

    @pl.when(m == 0)
    def _():
        act_all[0] = jnp.zeros((8, 32, 128), BF16)

    @pl.when(m == LINES - 1)
    def _():
        act_all[3] = jnp.zeros((8, 32, 128), BF16)

    position = lax.broadcasted_iota(jnp.int32, (256, 256), 0)
    channel = lax.broadcasted_iota(jnp.int32, (256, 256), 1)
    select = jnp.where(channel == (position % 32) * 8 + position // 32, 1.0, 0.0).astype(BF16)
    own_act.wait()
    turned = lax.dot_general(
        select, act_halo[1:3, 1].reshape(128, 256), (((1,), (1,)), ((), ())), preferred_element_type=F32
    )
    act_t[...] = turned.astype(BF16).reshape(8, 32, 128)
    own_grad.wait()

    has_outer = ((l == 0) & (m > 0)) | ((l == 1) & (m < LINES - 1))
    pl.semaphore_wait(barrier, 15 + LINES - 1 + jnp.where(has_outer, 16, 0))

    def grad_copy(k):
        peer = (l * 4 + h + k) % 8
        half = pl.multiple_of((peer % 4) // 2 * 128, 128)
        return pltpu.make_async_remote_copy(
            src_ref=grad_halo.at[pl.ds(1, 2), 1, :, pl.ds(half, 128)],
            dst_ref=grads.at[c, l, h],
            send_sem=g_send.at[k],
            recv_sem=g_recv.at[c],
            device_id=at(m, peer // 4, (peer % 4) * 2 + c),
            device_id_type=MESH,
        )

    def act_copy(k):
        peer = (n + k) % 16
        return pltpu.make_async_remote_copy(
            src_ref=act_t.at[(peer // 8) * 4 + peer % 4],
            dst_ref=act_all.at[1 + l, s],
            send_sem=act_send.at[k],
            recv_sem=act_recv.at[1 + l],
            device_id=at(m, peer // 8, peer % 8),
            device_id_type=MESH,
        )

    def outer_copy(k):
        peer = (n + k) % 16
        return pltpu.make_async_remote_copy(
            src_ref=act_t.at[(peer // 8) * 4 + peer % 4],
            dst_ref=act_all.at[3 - 3 * l, s],
            send_sem=act_send.at[16 + k],
            recv_sem=act_recv.at[3 - 3 * l],
            device_id=at(m - 1 + 2 * l, peer // 8, peer % 8),
            device_id_type=MESH,
        )

    own_half = pl.multiple_of(h // 2 * 128, 128)
    grad_here = pltpu.make_async_copy(
        grad_halo.at[pl.ds(1, 2), 1, :, pl.ds(own_half, 128)], grads.at[c, l, h], g_recv.at[c]
    )
    act_here = pltpu.make_async_copy(act_t.at[l * 4 + s % 4], act_all.at[1 + l, s], act_recv.at[1 + l])
    grad_here.start()
    act_here.start()

    def start(copy):
        def step(k, carry):
            copy(k).start()
            return carry
        return step

    def sent(copy):
        def step(k, carry):
            copy(k).wait_send()
            return carry
        return step

    lax.fori_loop(1, 8, start(grad_copy), 0)

    @pl.when(has_outer)
    def _():
        lax.fori_loop(0, 16, start(outer_copy), 0)

    lax.fori_loop(1, 16, start(act_copy), 0)

    pltpu.make_async_copy(grads.at[c], grads.at[c], g_recv.at[c]).wait()
    pass_on = pltpu.make_async_remote_copy(
        src_ref=grads.at[c],
        dst_ref=grads.at[c],
        send_sem=g_send.at[0],
        recv_sem=g_recv.at[c],
        device_id=(q, s + 1 - 2 * c),
        device_id_type=MESH,
    )
    pass_on.start()

    def build_rhs(core):
        def step(k, carry):
            side, depth = k // 4, k % 4
            block = grads[core, side, depth].astype(F32)
            base = pl.multiple_of((depth * 2 + core) * 256 + side * 128, 128)
            for tap, moved in enumerate((shifted(block, -1), block, shifted(block, 1))):
                rhs[pl.ds(base, 128), tap * 128 : (tap + 1) * 128] = moved.reshape(128, 128).astype(BF16)
            return carry
        lax.fori_loop(0, 8, step, 0)

    build_rhs(c)

    def halo_copies(index, halo):
        for dq in (-1, 0, 1):
            for ds in (-1, 0, 1):
                if dq == 0 and ds == 0:
                    continue
                number = index * 9 + (dq + 1) * 3 + ds + 1
                if ds == 0:
                    source, target = halo.at[pl.ds(1, 2), 1], halo.at[pl.ds(1, 2), 1 - dq]
                else:
                    source, target = halo.at[2 if ds == 1 else 1, 1], halo.at[0 if ds == 1 else 3, 1 - dq]
                there = (q + dq >= 0) & (q + dq < 2 * LINES) & (s + ds >= 0) & (s + ds < DEPTHS)
                comes = (q - dq >= 0) & (q - dq < 2 * LINES) & (s - ds >= 0) & (s - ds < DEPTHS)
                copy = functools.partial(
                    pltpu.make_async_remote_copy,
                    src_ref=source, dst_ref=target, send_sem=halo_send.at[number], recv_sem=halo_recv.at[number],
                    device_id=(q + dq, s + ds), device_id_type=MESH,
                )
                yield there, comes, copy

    both = ((0, act_halo), (1, grad_halo))
    for which in both:
        for there, _, copy in halo_copies(*which):
            pl.when(there)(lambda copy=copy: copy().start())

    for row in range(4):
        exists = (m > 0) if row == 0 else (m < LINES - 1) if row == 3 else (m >= 0)
        pl.when(exists)(pltpu.make_async_copy(act_all.at[row], act_all.at[row], act_recv.at[row]).wait)

    def build_lhs(k, carry):
        row, depth = k // 8, k % 8
        here = act_all[row, depth].astype(F32)
        before = act_all[row, jnp.maximum(depth - 1, 0)].astype(F32)
        after = act_all[row, jnp.minimum(depth + 1, DEPTHS - 1)].astype(F32)
        before = jnp.where(depth == 0, 0.0, before)
        after = jnp.where(depth == DEPTHS - 1, 0.0, after)
        low = lax.broadcasted_iota(jnp.int32, (32, 128), 1) < 64
        here_turned = pltpu.roll(here, 64, 1)
        down = jnp.where(low, pltpu.roll(before, 64, 1), here_turned).astype(BF16)
        up = jnp.where(low, here_turned, pltpu.roll(after, 64, 1)).astype(BF16)
        same = here.astype(BF16)
        for side in range(2):
            @pl.when((row - side >= 0) & (row - side < 3))
            def _(side=side):
                lanes = pl.ds(pl.multiple_of(depth * 256 + side * 128, 128), 128)
                for plane, value in enumerate((down, same, up)):
                    first = pl.multiple_of((plane * 3 + row - side) * 32, 32)
                    lhs[pl.ds(first, 32), lanes] = value
        return carry

    lax.fori_loop(0, 32, build_lhs, 0)

    pltpu.make_async_copy(grads.at[1 - c], grads.at[1 - c], g_recv.at[1 - c]).wait()
    build_rhs(1 - c)

    sums = jnp.dot(lhs[...], rhs[...], preferred_element_type=F32)
    for tap in range(3):
        product[tap] = sums[:, tap * 128 : (tap + 1) * 128]

    def build_message(k, carry):
        for tap in range(3):
            message[k, 8 * tap : 8 * tap + 8] = product[tap, pl.ds(k, 8, stride=32)]
            message[k, 24 + tap : 25 + tap] = product[tap, pl.ds(256 + k, 1)]
        return carry

    lax.fori_loop(0, LINES, build_message, 0)

    def line_copy(k):
        peer = (m + k) % LINES
        return pltpu.make_async_remote_copy(
            src_ref=message.at[peer],
            dst_ref=arrived.at[m],
            send_sem=b_send.at[k],
            recv_sem=b_recv,
            device_id=at(peer, l, s),
            device_id_type=MESH,
        )

    pltpu.make_async_copy(message.at[m], arrived.at[m], b_recv).start()
    lax.fori_loop(1, LINES, start(line_copy), 0)

    def convolve(halo, backward):
        total[...] = jnp.zeros_like(total)

        def step(k, carry):
            plane, row = k // 3, k % 3
            if backward:
                window = halo[pl.ds(2 - plane, 2), 2 - row]
            else:
                window = halo[pl.ds(plane, 2), row]
            window = window.reshape(128, 256)
            for tap in range(3):
                dims = (((1,), (1,)), ((), ())) if backward else (((1,), (0,)), ((), ()))
                total[tap] += lax.dot_general(window, w_v[k * 3 + tap], dims, preferred_element_type=F32)
            return carry

        lax.fori_loop(0, 9, step, 0)
        sums = [total[tap].reshape(2, 64, 256) for tap in range(3)]
        way = -1 if backward else 1
        return shifted(sums[0], way) + sums[1] + shifted(sums[2], -way)

    own_w.wait()
    for _, comes, copy in halo_copies(*both[0]):
        pl.when(comes)(lambda copy=copy: copy().wait_recv())
    out_ref[:, 0] = convolve(act_halo, False).astype(BF16)

    pltpu.make_async_copy(arrived, arrived, b_recv).wait()
    summed = arrived[0]
    for k in range(1, LINES):
        summed = summed + arrived[k]
    piece[...] = summed * (1.0 / 256.0)

    def depth_copy(k):
        return pltpu.make_async_remote_copy(
            src_ref=piece,
            dst_ref=pieces.at[s],
            send_sem=c_send.at[k],
            recv_sem=c_recv,
            device_id=(q, (s + k) % DEPTHS),
            device_id_type=MESH,
        )

    pltpu.make_async_copy(piece, pieces.at[s], c_recv).start()
    lax.fori_loop(1, DEPTHS, start(depth_copy), 0)

    for _, comes, copy in halo_copies(*both[1]):
        pl.when(comes)(lambda copy=copy: copy().wait_recv())
    gin_ref[:, 0] = convolve(grad_halo, True).astype(BF16)

    lax.fori_loop(1, 8, sent(grad_copy), 0)
    pass_on.wait_send()
    lax.fori_loop(1, 16, sent(act_copy), 0)

    @pl.when(has_outer)
    def _():
        lax.fori_loop(0, 16, sent(outer_copy), 0)

    for which in both:
        for there, _, copy in halo_copies(*which):
            pl.when(there)(lambda copy=copy: copy().wait_send())
    lax.fori_loop(1, LINES, sent(line_copy), 0)

    pltpu.make_async_copy(pieces, pieces, c_recv).wait()
    for depth in range(DEPTHS):
        half = depth // 4
        for tap in range(3):
            first = 4 * tap + depth % 4
            mixed[half, pl.ds(first, 8, stride=12)] = pieces[depth, 8 * tap : 8 * tap + 8]
            mixed[half, 96 + first : 97 + first] = pieces[depth, 24 + tap : 25 + tap]
    for half in range(2):
        gw_ref[:, half * 128 : (half + 1) * 128] = mixed[half]
    lax.fori_loop(1, DEPTHS, sent(depth_copy), 0)


def on_device(activations, weights, grad_output):
    vmem = pl.BlockSpec(memory_space=pltpu.VMEM)
    dma = pltpu.SemaphoreType.DMA
    output, grad_input, grad_weights = pl.pallas_call(
        kernel,
        out_shape=(
            jax.ShapeDtypeStruct((2, 1, 64, 256), BF16),
            jax.ShapeDtypeStruct((2, 1, 64, 256), BF16),
            jax.ShapeDtypeStruct((108, 256), F32),
        ),
        in_specs=[pl.BlockSpec(memory_space=pl.ANY)] * 3,
        out_specs=(vmem, vmem, vmem),
        scratch_shapes=[
            pltpu.VMEM((4, 3, 64, 256), BF16),
            pltpu.VMEM((4, 3, 64, 256), BF16),
            pltpu.VMEM((27, 256, 256), BF16),
            pltpu.VMEM((8, 32, 128), BF16),
            pltpu.VMEM((4, 8, 32, 128), BF16),
            pltpu.VMEM((2, 2, 4, 2, 64, 128), BF16),
            pltpu.VMEM((288, 2048), BF16),
            pltpu.VMEM((2048, 384), BF16),
            pltpu.VMEM((3, 288, 128), F32),
            pltpu.VMEM((LINES, 27, 128), F32),
            pltpu.VMEM((LINES, 27, 128), F32),
            pltpu.VMEM((27, 128), F32),
            pltpu.VMEM((DEPTHS, 27, 128), F32),
            pltpu.VMEM((2, 108, 128), F32),
            pltpu.VMEM((3, 128, 256), F32),
            dma((3,)),
            dma((32,)),
            dma((4,)),
            dma((8,)),
            dma((2,)),
            dma((LINES,)),
            dma(()),
            dma((DEPTHS,)),
            dma(()),
            dma((18,)),
            dma((18,)),
        ],
        compiler_params=pltpu.CompilerParams(
            collective_id=0, has_side_effects=True, vmem_limit_bytes=40 << 20
        ),
    )(activations, weights, grad_output)
    return output, grad_input, grad_weights.reshape(27, 4, 256)


def solution(mesh):
    return jax.shard_map(
        on_device,
        mesh=mesh,
        in_specs=(P("sp", "chan", None, None), P(), P("sp", "chan", None, None)),
        out_specs=(P("sp", "chan", None, None), P("sp", "chan", None, None), P(None, "chan", None)),
        check_vma=False,
    )
```

```python
import functools

import jax
import jax.numpy as jnp
from jax import lax
from jax.experimental import pallas as pl
from jax.experimental.pallas import tpu as pltpu
from jax.sharding import PartitionSpec as P

MESH = pl.DeviceIdType.MESH
F32 = jnp.float32
BF16 = jnp.bfloat16

LINES = 32
DEPTHS = 8
ROW_ORDER = (1, 0, 2)


def shifted(value, by):
    width = value.shape[-2]
    rolled = pltpu.roll(value, by % width, value.ndim - 2)
    place = lax.broadcasted_iota(jnp.int32, value.shape, value.ndim - 2)
    return jnp.where(place == (0 if by == 1 else width - 1), 0.0, rolled)


def kernel(
    act_hbm, w_hbm, grad_hbm, out_ref, gin_ref, pieces,
    act_halo, grad_halo, w_v, act_t, act_all, grads, lhs, rhs, product, centre, sides, centre_in, sides_in, piece, total,
    in_sem, act_send, act_recv, g_send, g_recv, b_send, b_recv, c_send, c_recv, halo_send, halo_recv,
):
    q, s = lax.axis_index("chan"), lax.axis_index("sp")
    m, l = q // 2, q % 2
    h, c = s // 2, s % 2

    def at(line, side, depth):
        return (line * 2 + side, depth)

    own_grad = pltpu.make_async_copy(grad_hbm.at[:, 0], grad_halo.at[pl.ds(1, 2), 1], in_sem.at[0])
    own_act = pltpu.make_async_copy(act_hbm.at[:, 0], act_halo.at[pl.ds(1, 2), 1], in_sem.at[1])
    own_w = pltpu.make_async_copy(w_hbm, w_v, in_sem.at[2])
    own_grad.start()
    own_act.start()
    own_w.start()

    barrier = pltpu.get_barrier_semaphore()

    def greet(device):
        pl.semaphore_signal(barrier, inc=1, device_id=device, device_id_type=MESH)

    n = l * 8 + s

    def greet_line(k, carry):
        peer = (n + k) % 16
        greet(at(m, peer // 8, peer % 8))
        return carry

    lax.fori_loop(1, 16, greet_line, 0)

    @pl.when(m > 0)
    def _():
        lax.fori_loop(0, DEPTHS, lambda k, t: (greet(at(m - 1, 1, k)), t)[1], 0)

    @pl.when(m < LINES - 1)
    def _():
        lax.fori_loop(0, DEPTHS, lambda k, t: (greet(at(m + 1, 0, k)), t)[1], 0)

    def greet_plane(k, carry):
        greet(at((m + k) % LINES, l, s))
        return carry

    lax.fori_loop(1, LINES, greet_plane, 0)

    for halo in (act_halo, grad_halo):
        @pl.when(q == 0)
        def _(halo=halo):
            halo[1:3, 0] = jnp.zeros((2, 64, 256), BF16)

        @pl.when(q == 2 * LINES - 1)
        def _(halo=halo):
            halo[1:3, 2] = jnp.zeros((2, 64, 256), BF16)

        @pl.when(s == 0)
        def _(halo=halo):
            halo[0] = jnp.zeros((3, 64, 256), BF16)

        @pl.when(s == DEPTHS - 1)
        def _(halo=halo):
            halo[3] = jnp.zeros((3, 64, 256), BF16)

    @pl.when(m == 0)
    def _():
        act_all[0] = jnp.zeros((8, 32, 128), BF16)

    @pl.when(m == LINES - 1)
    def _():
        act_all[3] = jnp.zeros((8, 32, 128), BF16)

    position = lax.broadcasted_iota(jnp.int32, (256, 256), 0)
    channel = lax.broadcasted_iota(jnp.int32, (256, 256), 1)
    select = jnp.where(channel == (position % 32) * 8 + position // 32, 1.0, 0.0).astype(BF16)
    own_act.wait()
    turned = lax.dot_general(
        select, act_halo[1:3, 1].reshape(128, 256), (((1,), (1,)), ((), ())), preferred_element_type=F32
    )
    act_t[...] = turned.astype(BF16).reshape(8, 32, 128)
    own_grad.wait()

    has_outer = ((l == 0) & (m > 0)) | ((l == 1) & (m < LINES - 1))
    pl.semaphore_wait(barrier, 15 + LINES - 1 + jnp.where(has_outer, 16, 0))

    def halo_copy(halo, number, source, target, device):
        return functools.partial(
            pltpu.make_async_remote_copy,
            src_ref=source, dst_ref=target, send_sem=halo_send.at[number], recv_sem=halo_recv.at[number],
            device_id=device, device_id_type=MESH,
        )

    def row_copies(index, halo):
        for place, dq in enumerate((-1, 1)):
            source, target = halo.at[pl.ds(1, 2), 1], halo.at[pl.ds(1, 2), 1 - dq]
            copy = halo_copy(halo, 4 * index + place, source, target, (q + dq, s))
            yield (q + dq >= 0) & (q + dq < 2 * LINES), (q - dq >= 0) & (q - dq < 2 * LINES), copy

    def plane_copies(index, halo):
        for place, ds in enumerate((-1, 1)):
            source, target = halo.at[1 if ds == -1 else 2], halo.at[3 if ds == -1 else 0]
            copy = halo_copy(halo, 4 * index + 2 + place, source, target, (q, s + ds))
            yield (s + ds >= 0) & (s + ds < DEPTHS), (s - ds >= 0) & (s - ds < DEPTHS), copy

    both = ((0, act_halo), (1, grad_halo))

    def convolve(index, halo, planes):
        for tap in range(3):
            part = 0.0 if len(planes) == 1 else total[index, tap]
            for plane in planes:
                for row in range(3):
                    weight = w_v[(plane * 3 + row) * 3 + tap]
                    if index:
                        window, dims = halo[2 - plane : 4 - plane, 2 - row], (((1,), (1,)), ((), ()))
                    else:
                        window, dims = halo[plane : plane + 2, row], (((1,), (0,)), ((), ()))
                    part += lax.dot_general(window.reshape(128, 256), weight, dims, preferred_element_type=F32)
            total[index, tap] = part

    def joined(index):
        sums = [total[index, tap].reshape(2, 64, 256) for tap in range(3)]
        way = -1 if index else 1
        return (shifted(sums[0], way) + sums[1] + shifted(sums[2], -way)).astype(BF16)

    def grad_copy(k):
        peer = (l * 4 + h + k) % 8
        half = pl.multiple_of((peer % 4) // 2 * 128, 128)
        return pltpu.make_async_remote_copy(
            src_ref=grad_halo.at[pl.ds(1, 2), 1, :, pl.ds(half, 128)],
            dst_ref=grads.at[c, l, h],
            send_sem=g_send.at[k],
            recv_sem=g_recv.at[c],
            device_id=at(m, peer // 4, (peer % 4) * 2 + c),
            device_id_type=MESH,
        )

    def act_copy(k):
        peer = (n + k) % 16
        return pltpu.make_async_remote_copy(
            src_ref=act_t.at[(peer // 8) * 4 + peer % 4],
            dst_ref=act_all.at[1 + l, s],
            send_sem=act_send.at[k],
            recv_sem=act_recv.at[1 + l],
            device_id=at(m, peer // 8, peer % 8),
            device_id_type=MESH,
        )

    def outer_copy(k):
        peer = (n + k) % 16
        return pltpu.make_async_remote_copy(
            src_ref=act_t.at[(peer // 8) * 4 + peer % 4],
            dst_ref=act_all.at[3 - 3 * l, s],
            send_sem=act_send.at[16 + k],
            recv_sem=act_recv.at[3 - 3 * l],
            device_id=at(m - 1 + 2 * l, peer // 8, peer % 8),
            device_id_type=MESH,
        )

    own_half = pl.multiple_of(h // 2 * 128, 128)
    grad_here = pltpu.make_async_copy(
        grad_halo.at[pl.ds(1, 2), 1, :, pl.ds(own_half, 128)], grads.at[c, l, h], g_recv.at[c]
    )
    act_here = pltpu.make_async_copy(act_t.at[l * 4 + s % 4], act_all.at[1 + l, s], act_recv.at[1 + l])
    grad_here.start()
    act_here.start()

    def start(copy):
        def step(k, carry):
            copy(k).start()
            return carry
        return step

    def sent(copy):
        def step(k, carry):
            copy(k).wait_send()
            return carry
        return step

    lax.fori_loop(1, 8, start(grad_copy), 0)

    lax.fori_loop(1, 16, start(act_copy), 0)

    @pl.when(has_outer)
    def _():
        lax.fori_loop(0, 16, start(outer_copy), 0)

    pltpu.make_async_copy(grads.at[c], grads.at[c], g_recv.at[c]).wait()
    pass_on = pltpu.make_async_remote_copy(
        src_ref=grads.at[c],
        dst_ref=grads.at[c],
        send_sem=g_send.at[0],
        recv_sem=g_recv.at[c],
        device_id=(q, s + 1 - 2 * c),
        device_id_type=MESH,
    )
    pass_on.start()

    def build_rhs(core):
        for side in range(2):
            for depth in range(4):
                block = grads[core, side, depth].astype(F32)
                base = pl.multiple_of(core * 256 + depth * 512 + side * 128, 128)
                for tap, moved in enumerate((shifted(block, -1), block, shifted(block, 1))):
                    rhs[pl.ds(base, 128), tap * 128 : (tap + 1) * 128] = moved.reshape(128, 128).astype(BF16)

    build_rhs(c)

    pltpu.make_async_copy(grads.at[1 - c], grads.at[1 - c], g_recv.at[1 - c]).wait()
    build_rhs(1 - c)

    def build_lhs(row, sides):
        here = act_all[row].astype(F32)
        turned = pltpu.roll(here, 64, 2)
        nothing = jnp.zeros((1, 32, 128), F32)
        low = lax.broadcasted_iota(jnp.int32, (8, 32, 128), 2) < 64
        down = jnp.where(low, jnp.concatenate([nothing, turned[:-1]]), turned).astype(BF16)
        up = jnp.where(low, turned, jnp.concatenate([turned[1:], nothing])).astype(BF16)
        for plane, value in enumerate((down, act_all[row], up)):
            for side in sides:
                first = (ROW_ORDER.index(row - side) * 3 + plane) * 32
                for depth in range(DEPTHS):
                    lane = depth * 256 + side * 128
                    lhs[first : first + 32, lane : lane + 128] = value[depth]

    def arrival(row):
        return pltpu.make_async_copy(act_all.at[row], act_all.at[row], act_recv.at[row])

    def multiply(first, last):
        sums = jnp.dot(lhs[first:last], rhs[...], preferred_element_type=F32)
        for tap in range(3):
            product[tap, first:last] = sums[:, tap * 128 : (tap + 1) * 128]

    def line_copy(buffer, landing, number):
        def copy(k):
            peer = (m + k) % LINES
            return pltpu.make_async_remote_copy(
                src_ref=buffer.at[peer],
                dst_ref=landing.at[m],
                send_sem=b_send.at[number * LINES + k],
                recv_sem=b_recv.at[number],
                device_id=at(peer, l, s),
                device_id_type=MESH,
            )
        return copy

    centre_copy, sides_copy = line_copy(centre, centre_in, 0), line_copy(sides, sides_in, 1)

    arrival(1).wait()
    build_lhs(1, (0, 1))
    arrival(2).wait()
    build_lhs(2, (0, 1))
    multiply(0, 96)
    for k in range(LINES):
        for tap in range(3):
            centre[k, 3 * tap : 3 * tap + 3] = product[tap, pl.ds(k, 3, stride=32)]
    pltpu.make_async_copy(centre.at[m], centre_in.at[m], b_recv.at[0]).start()
    lax.fori_loop(1, LINES, start(centre_copy), 0)

    pl.when(m > 0)(arrival(0).wait)
    build_lhs(0, (0,))
    pl.when(m < LINES - 1)(arrival(3).wait)
    build_lhs(3, (1,))
    for which in both:
        for there, _, copy in row_copies(*which):
            pl.when(there)(lambda copy=copy: copy().start())
    multiply(96, 288)
    for k in range(LINES):
        for tap in range(3):
            sides[k, 6 * tap : 6 * tap + 6] = product[tap, pl.ds(96 + k, 6, stride=32)]
    pltpu.make_async_copy(sides.at[m], sides_in.at[m], b_recv.at[1]).start()
    lax.fori_loop(1, LINES, start(sides_copy), 0)

    own_w.wait()
    for which in both:
        for _, comes, copy in row_copies(*which):
            pl.when(comes)(lambda copy=copy: copy().wait_recv())
        for there, _, copy in plane_copies(*which):
            pl.when(there)(lambda copy=copy: copy().start())
    for which in both:
        convolve(*which, (1,))
    for _, comes, copy in plane_copies(*both[0]):
        pl.when(comes)(lambda copy=copy: copy().wait_recv())
    convolve(*both[0], (0, 2))
    out_ref[:, 0] = joined(0)

    pltpu.make_async_copy(centre_in, centre_in, b_recv.at[0]).wait()
    piece[0:9] = sum(centre_in[k] for k in range(LINES)) * (1.0 / 256.0)
    pltpu.make_async_copy(sides_in, sides_in, b_recv.at[1]).wait()
    piece[9:27] = sum(sides_in[k] for k in range(LINES)) * (1.0 / 256.0)

    def depth_copy(k):
        return pltpu.make_async_remote_copy(
            src_ref=piece,
            dst_ref=pieces.at[s],
            send_sem=c_send.at[k],
            recv_sem=c_recv,
            device_id=(q, (s + k) % DEPTHS),
            device_id_type=MESH,
        )

    pltpu.make_async_copy(piece, pieces.at[s], c_recv).start()
    lax.fori_loop(1, DEPTHS, start(depth_copy), 0)

    for _, comes, copy in plane_copies(*both[1]):
        pl.when(comes)(lambda copy=copy: copy().wait_recv())
    convolve(*both[1], (0, 2))
    gin_ref[:, 0] = joined(1)

    lax.fori_loop(1, 8, sent(grad_copy), 0)
    pass_on.wait_send()
    lax.fori_loop(1, 16, sent(act_copy), 0)

    @pl.when(has_outer)
    def _():
        lax.fori_loop(0, 16, sent(outer_copy), 0)

    for which in both:
        for copies in (row_copies, plane_copies):
            for there, _, copy in copies(*which):
                pl.when(there)(lambda copy=copy: copy().wait_send())
    lax.fori_loop(1, LINES, sent(centre_copy), 0)
    lax.fori_loop(1, LINES, sent(sides_copy), 0)

    pltpu.make_async_copy(pieces, pieces, c_recv).wait()
    lax.fori_loop(1, DEPTHS, sent(depth_copy), 0)


def finish(out_v, gin_v, pieces, out_hbm, gin_hbm, gw_hbm, mixed, together, sem):
    out_copy = pltpu.make_async_copy(out_v, out_hbm, sem.at[0])
    gin_copy = pltpu.make_async_copy(gin_v, gin_hbm, sem.at[1])
    out_copy.start()
    gin_copy.start()
    for depth in range(DEPTHS):
        half = depth // 4
        for tap in range(3):
            for index, row in enumerate(ROW_ORDER):
                first = (3 * row + tap) * 4 + depth % 4
                start = 6 + 6 * tap + 3 * index if index else 3 * tap
                mixed[half, pl.ds(first, 3, stride=36)] = pieces[depth, start : start + 3]
    for half in range(2):
        together[:, :, half * 128 : (half + 1) * 128] = mixed[half].reshape(27, 4, 128)
    gw_copy = pltpu.make_async_copy(together, gw_hbm, sem.at[2])
    gw_copy.start()
    out_copy.wait()
    gin_copy.wait()
    gw_copy.wait()


def on_device(activations, weights, grad_output):
    vmem = pl.BlockSpec(memory_space=pltpu.VMEM)
    dma = pltpu.SemaphoreType.DMA
    hbm = pl.BlockSpec(memory_space=pltpu.HBM)
    output, grad_input, pieces = pl.pallas_call(
        kernel,
        out_shape=(
            jax.ShapeDtypeStruct((2, 1, 64, 256), BF16),
            jax.ShapeDtypeStruct((2, 1, 64, 256), BF16),
            jax.ShapeDtypeStruct((DEPTHS, 27, 128), F32),
        ),
        in_specs=[hbm] * 3,
        out_specs=(vmem, vmem, vmem),
        scratch_shapes=[
            pltpu.VMEM((4, 3, 64, 256), BF16),
            pltpu.VMEM((4, 3, 64, 256), BF16),
            pltpu.VMEM((27, 256, 256), BF16),
            pltpu.VMEM((8, 32, 128), BF16),
            pltpu.VMEM((4, 8, 32, 128), BF16),
            pltpu.VMEM((2, 2, 4, 2, 64, 128), BF16),
            pltpu.VMEM((288, 2048), BF16),
            pltpu.VMEM((2048, 384), BF16),
            pltpu.VMEM((3, 288, 128), F32),
            pltpu.VMEM((LINES, 9, 128), F32),
            pltpu.VMEM((LINES, 18, 128), F32),
            pltpu.VMEM((LINES, 9, 128), F32),
            pltpu.VMEM((LINES, 18, 128), F32),
            pltpu.VMEM((27, 128), F32),
            pltpu.VMEM((2, 3, 128, 256), F32),
            dma((3,)),
            dma((32,)),
            dma((4,)),
            dma((8,)),
            dma((2,)),
            dma((2 * LINES,)),
            dma((2,)),
            dma((DEPTHS,)),
            dma(()),
            dma((8,)),
            dma((8,)),
        ],
        compiler_params=pltpu.CompilerParams(
            collective_id=0, has_side_effects=True, vmem_limit_bytes=40 << 20
        ),
    )(*(pltpu.with_memory_space_constraint(operand, pltpu.HBM) for operand in (activations, weights, grad_output)))
    return pl.pallas_call(
        finish,
        out_shape=(
            jax.ShapeDtypeStruct((2, 1, 64, 256), BF16),
            jax.ShapeDtypeStruct((2, 1, 64, 256), BF16),
            jax.ShapeDtypeStruct((27, 4, 256), F32),
        ),
        in_specs=[vmem] * 3,
        out_specs=(hbm, hbm, hbm),
        scratch_shapes=[pltpu.VMEM((2, 108, 128), F32), pltpu.VMEM((27, 4, 256), F32), dma((3,))],
        compiler_params=pltpu.CompilerParams(vmem_limit_bytes=8 << 20),
    )(output, grad_input, pieces)


def solution(mesh):
    return jax.shard_map(
        on_device,
        mesh=mesh,
        in_specs=(P("sp", "chan", None, None), P(), P("sp", "chan", None, None)),
        out_specs=(P("sp", "chan", None, None), P("sp", "chan", None, None), P(None, "chan", None)),
        check_vma=False,
    )
```

```python
import functools

import jax
import jax.numpy as jnp
from jax import lax
from jax.experimental import pallas as pl
from jax.experimental.pallas import tpu as pltpu
from jax.sharding import PartitionSpec as P

MESH = pl.DeviceIdType.MESH
F32 = jnp.float32
BF16 = jnp.bfloat16

LINES = 32
DEPTHS = 8
ROW_ORDER = (1, 0, 2)


def shifted(value, by):
    width = value.shape[-2]
    rolled = pltpu.roll(value, by % width, value.ndim - 2)
    place = lax.broadcasted_iota(jnp.int32, value.shape, value.ndim - 2)
    return jnp.where(place == (0 if by == 1 else width - 1), 0.0, rolled)


def kernel(
    act_hbm, w_hbm, grad_hbm, out_ref, gin_ref, centre_out, sides_out,
    act_halo, grad_halo, w_v, act_t, act_all, grads, lhs, rhs, product, centre, sides, centre_in, sides_in, centre_sum, sides_sum, total,
    in_sem, act_send, act_recv, g_send, g_recv, b_send, b_recv, c_send, c_recv, halo_send, halo_recv,
):
    q, s = lax.axis_index("chan"), lax.axis_index("sp")
    m, l = q // 2, q % 2
    h, c = s // 2, s % 2

    z = 2 * h + l

    def at(line, side, depth):
        return (line * 2 + side, depth)

    def away(k, count):
        return count // 2 + jnp.where(k % 2 == 0, k // 2, -((k + 1) // 2))

    own_grad = pltpu.make_async_copy(grad_hbm.at[:, 0], grad_halo.at[pl.ds(1, 2), 1], in_sem.at[0])
    own_act = pltpu.make_async_copy(act_hbm.at[:, 0], act_halo.at[pl.ds(1, 2), 1], in_sem.at[1])
    own_w = pltpu.make_async_copy(w_hbm, w_v, in_sem.at[2])
    own_grad.start()
    own_act.start()
    own_w.start()

    barrier = pltpu.get_barrier_semaphore()

    def greet(device):
        pl.semaphore_signal(barrier, inc=1, device_id=device, device_id_type=MESH)

    n = l * 8 + s

    def greet_line(k, carry):
        peer = (n + k) % 16
        greet(at(m, peer // 8, peer % 8))
        return carry

    lax.fori_loop(1, 16, greet_line, 0)

    @pl.when(m > 0)
    def _():
        lax.fori_loop(0, DEPTHS, lambda k, t: (greet(at(m - 1, 1, k)), t)[1], 0)

    @pl.when(m < LINES - 1)
    def _():
        lax.fori_loop(0, DEPTHS, lambda k, t: (greet(at(m + 1, 0, k)), t)[1], 0)

    def greet_plane(k, carry):
        greet(at((m + k) % LINES, l, s))
        return carry

    lax.fori_loop(1, LINES, greet_plane, 0)

    for halo in (act_halo, grad_halo):
        @pl.when(q == 0)
        def _(halo=halo):
            halo[1:3, 0] = jnp.zeros((2, 64, 256), BF16)

        @pl.when(q == 2 * LINES - 1)
        def _(halo=halo):
            halo[1:3, 2] = jnp.zeros((2, 64, 256), BF16)

        @pl.when(s == 0)
        def _(halo=halo):
            halo[0] = jnp.zeros((3, 64, 256), BF16)

        @pl.when(s == DEPTHS - 1)
        def _(halo=halo):
            halo[3] = jnp.zeros((3, 64, 256), BF16)

    @pl.when(m == 0)
    def _():
        act_all[0] = jnp.zeros((8, 32, 128), BF16)

    @pl.when(m == LINES - 1)
    def _():
        act_all[3] = jnp.zeros((8, 32, 128), BF16)

    position = lax.broadcasted_iota(jnp.int32, (256, 256), 0)
    channel = lax.broadcasted_iota(jnp.int32, (256, 256), 1)
    select = jnp.where(channel == (position % 32) * 8 + position // 32, 1.0, 0.0).astype(BF16)
    own_act.wait()
    turned = lax.dot_general(
        select, act_halo[1:3, 1].reshape(128, 256), (((1,), (1,)), ((), ())), preferred_element_type=F32
    )
    act_t[...] = turned.astype(BF16).reshape(8, 32, 128)
    has_outer = ((l == 0) & (m > 0)) | ((l == 1) & (m < LINES - 1))
    pl.semaphore_wait(barrier, 15 + LINES - 1 + jnp.where(has_outer, 16, 0))

    def halo_copy(halo, number, source, target, device):
        return functools.partial(
            pltpu.make_async_remote_copy,
            src_ref=source, dst_ref=target, send_sem=halo_send.at[number], recv_sem=halo_recv.at[number],
            device_id=device, device_id_type=MESH,
        )

    def row_copies(index, halo):
        for place, dq in enumerate((-1, 1)):
            source, target = halo.at[pl.ds(1, 2), 1], halo.at[pl.ds(1, 2), 1 - dq]
            copy = halo_copy(halo, 4 * index + place, source, target, (q + dq, s))
            yield (q + dq >= 0) & (q + dq < 2 * LINES), (q - dq >= 0) & (q - dq < 2 * LINES), copy

    def plane_copies(index, halo):
        for place, ds in enumerate((-1, 1)):
            source, target = halo.at[1 if ds == -1 else 2], halo.at[3 if ds == -1 else 0]
            copy = halo_copy(halo, 4 * index + 2 + place, source, target, (q, s + ds))
            yield (s + ds >= 0) & (s + ds < DEPTHS), (s - ds >= 0) & (s - ds < DEPTHS), copy

    both = ((0, act_halo), (1, grad_halo))

    def convolve(index, halo, planes):
        for tap in range(3):
            part = 0.0 if len(planes) == 1 else total[index, tap]
            for plane in planes:
                for row in range(3):
                    weight = w_v[(plane * 3 + row) * 3 + tap]
                    if index:
                        window, dims = halo[2 - plane : 4 - plane, 2 - row], (((1,), (1,)), ((), ()))
                    else:
                        window, dims = halo[plane : plane + 2, row], (((1,), (0,)), ((), ()))
                    part += lax.dot_general(window.reshape(128, 256), weight, dims, preferred_element_type=F32)
            total[index, tap] = part

    def joined(index):
        sums = [total[index, tap].reshape(2, 64, 256) for tap in range(3)]
        way = -1 if index else 1
        return (shifted(sums[0], way) + sums[1] + shifted(sums[2], -way)).astype(BF16)

    def grad_copy(k):
        there = (z + away(k, 8)) % 8
        half = pl.multiple_of(there // 4 * 128, 128)
        return pltpu.make_async_remote_copy(
            src_ref=grad_hbm.at[:, 0, :, pl.ds(half, 128)],
            dst_ref=grads.at[c, l, h],
            send_sem=g_send.at[k],
            recv_sem=g_recv.at[c],
            device_id=at(m, there % 2, there // 2 * 2 + c),
            device_id_type=MESH,
        )

    def in_line(k):
        there = (z + away(k // 2, 8)) % 8
        return there % 2, there // 2 * 2 + (c + 1 + k) % 2

    def act_copy(k):
        side, depth = in_line(k)
        return pltpu.make_async_remote_copy(
            src_ref=act_t.at[side * 4 + depth % 4],
            dst_ref=act_all.at[1 + l, s],
            send_sem=act_send.at[k],
            recv_sem=act_recv.at[1 + l],
            device_id=at(m, side, depth),
            device_id_type=MESH,
        )

    def outer_copy(k):
        side, depth = in_line(k)
        return pltpu.make_async_remote_copy(
            src_ref=act_t.at[side * 4 + depth % 4],
            dst_ref=act_all.at[3 - 3 * l, s],
            send_sem=act_send.at[16 + k],
            recv_sem=act_recv.at[3 - 3 * l],
            device_id=at(m - 1 + 2 * l, side, depth),
            device_id_type=MESH,
        )

    own_half = pl.multiple_of(h // 2 * 128, 128)
    grad_here = pltpu.make_async_copy(
        grad_hbm.at[:, 0, :, pl.ds(own_half, 128)], grads.at[c, l, h], g_recv.at[c]
    )
    act_here = pltpu.make_async_copy(act_t.at[l * 4 + s % 4], act_all.at[1 + l, s], act_recv.at[1 + l])
    grad_here.start()

    def start(copy):
        def step(k, carry):
            copy(k).start()
            return carry
        return step

    def sent(copy):
        def step(k, carry):
            copy(k).wait_send()
            return carry
        return step

    lax.fori_loop(0, 7, start(grad_copy), 0)

    act_here.start()
    lax.fori_loop(0, 15, start(act_copy), 0)

    @pl.when(has_outer)
    def _():
        lax.fori_loop(0, 16, start(outer_copy), 0)

    pltpu.make_async_copy(grads.at[c], grads.at[c], g_recv.at[c]).wait()
    pass_on = pltpu.make_async_remote_copy(
        src_ref=grads.at[c],
        dst_ref=grads.at[c],
        send_sem=g_send.at[7],
        recv_sem=g_recv.at[c],
        device_id=(q, s + 1 - 2 * c),
        device_id_type=MESH,
    )
    pass_on.start()

    def build_rhs(core):
        for side in range(2):
            for depth in range(4):
                block = grads[core, side, depth].astype(F32)
                base = pl.multiple_of(core * 128 + depth * 256 + side * 1024, 128)
                for tap, moved in enumerate((shifted(block, -1), block, shifted(block, 1))):
                    rhs[pl.ds(base, 128), tap * 128 : (tap + 1) * 128] = moved.reshape(128, 128).astype(BF16)

    build_rhs(c)

    pltpu.make_async_copy(grads.at[1 - c], grads.at[1 - c], g_recv.at[1 - c]).wait()
    build_rhs(1 - c)

    def build_lhs(row, sides):
        here = act_all[row].astype(F32)
        turned = pltpu.roll(here, 64, 2)
        nothing = jnp.zeros((1, 32, 128), F32)
        low = lax.broadcasted_iota(jnp.int32, (8, 32, 128), 2) < 64
        down = jnp.where(low, jnp.concatenate([nothing, turned[:-1]]), turned).astype(BF16)
        up = jnp.where(low, turned, jnp.concatenate([turned[1:], nothing])).astype(BF16)
        for plane, value in enumerate((down, act_all[row], up)):
            for side in sides:
                first = (ROW_ORDER.index(row - side) * 3 + plane) * 32
                for depth in range(DEPTHS):
                    lane = depth * 128 + side * 1024
                    lhs[first : first + 32, lane : lane + 128] = value[depth]

    def arrival(row):
        return pltpu.make_async_copy(act_all.at[row], act_all.at[row], act_recv.at[row])

    def multiply(rows, cells):
        sums = jnp.dot(lhs[rows, cells], rhs[cells], preferred_element_type=F32)
        return [sums[:, tap * 128 : (tap + 1) * 128] for tap in range(3)]

    def line_copy(buffer, landing, number):
        def copy(k):
            peer = (m // 8 + away(k % 4, 4)) % 4 * 8 + (m + away(k // 4, 8)) % 8
            return pltpu.make_async_remote_copy(
                src_ref=buffer.at[peer],
                dst_ref=landing.at[m],
                send_sem=b_send.at[number * LINES + k],
                recv_sem=b_recv.at[number],
                device_id=at(peer, l, s),
                device_id_type=MESH,
            )
        return copy

    centre_copy, sides_copy = line_copy(centre, centre_in, 0), line_copy(sides, sides_in, 1)

    own_grad.wait()
    for which in both:
        for there, _, copy in row_copies(*which):
            pl.when(there)(lambda copy=copy: copy().start())

    arrival(1).wait()
    build_lhs(1, (0, 1))
    arrival(2).wait()
    build_lhs(2, (0, 1))
    for tap, part in enumerate(multiply(slice(0, 96), slice(None))):
        product[tap, 0:96] = part
    for k in range(LINES):
        for tap in range(3):
            centre[k, 3 * tap : 3 * tap + 3] = product[tap, pl.ds(k, 3, stride=32)]
    pltpu.make_async_copy(centre.at[m], centre_in.at[m], b_recv.at[0]).start()
    lax.fori_loop(0, LINES - 1, start(centre_copy), 0)

    low_cells, high_cells = slice(0, 1024), slice(1024, 2048)
    for tap, part in enumerate(multiply(slice(96, 192), high_cells)):
        product[tap, 96:192] = part
    for tap, part in enumerate(multiply(slice(192, 288), low_cells)):
        product[tap, 192:288] = part
    pl.when(m > 0)(arrival(0).wait)
    build_lhs(0, (0,))
    pl.when(m < LINES - 1)(arrival(3).wait)
    build_lhs(3, (1,))
    for tap, part in enumerate(multiply(slice(96, 192), low_cells)):
        product[tap, 96:192] += part
    for tap, part in enumerate(multiply(slice(192, 288), high_cells)):
        product[tap, 192:288] += part
    for k in range(LINES):
        for tap in range(3):
            sides[k, 6 * tap : 6 * tap + 6] = product[tap, pl.ds(96 + k, 6, stride=32)]
    pltpu.make_async_copy(sides.at[m], sides_in.at[m], b_recv.at[1]).start()
    lax.fori_loop(0, LINES - 1, start(sides_copy), 0)

    own_w.wait()
    for which in both:
        for _, comes, copy in row_copies(*which):
            pl.when(comes)(lambda copy=copy: copy().wait_recv())
        for there, _, copy in plane_copies(*which):
            pl.when(there)(lambda copy=copy: copy().start())
    for which in both:
        convolve(*which, (1,))
    for _, comes, copy in plane_copies(*both[0]):
        pl.when(comes)(lambda copy=copy: copy().wait_recv())
    convolve(*both[0], (0, 2))
    out_ref[:, 0] = joined(0)

    def depth_copy(mine, landing, number):
        def copy(k):
            there = (h + away(k // 2, 4)) % 4
            return pltpu.make_async_remote_copy(
                src_ref=mine,
                dst_ref=landing.at[s],
                send_sem=c_send.at[number * DEPTHS + k],
                recv_sem=c_recv.at[number],
                device_id=(q, there * 2 + (c + 1 + k) % 2),
                device_id_type=MESH,
            )
        return copy

    gathers = []
    for number, (summands, mine, landing) in enumerate(
        ((centre_in, centre_sum, centre_out), (sides_in, sides_sum, sides_out))
    ):
        pltpu.make_async_copy(summands, summands, b_recv.at[number]).wait()
        mine[...] = sum(summands[k] for k in range(LINES)) * (1.0 / 256.0)
        pltpu.make_async_copy(mine, landing.at[s], c_recv.at[number]).start()
        gathers.append(depth_copy(mine, landing, number))
        lax.fori_loop(0, DEPTHS - 1, start(gathers[number]), 0)

    for _, comes, copy in plane_copies(*both[1]):
        pl.when(comes)(lambda copy=copy: copy().wait_recv())
    convolve(*both[1], (0, 2))
    gin_ref[:, 0] = joined(1)

    lax.fori_loop(0, 7, sent(grad_copy), 0)
    pass_on.wait_send()
    lax.fori_loop(0, 15, sent(act_copy), 0)

    @pl.when(has_outer)
    def _():
        lax.fori_loop(0, 16, sent(outer_copy), 0)

    for which in both:
        for copies in (row_copies, plane_copies):
            for there, _, copy in copies(*which):
                pl.when(there)(lambda copy=copy: copy().wait_send())
    lax.fori_loop(0, LINES - 1, sent(centre_copy), 0)
    lax.fori_loop(0, LINES - 1, sent(sides_copy), 0)

    for number, landing in enumerate((centre_out, sides_out)):
        pltpu.make_async_copy(landing, landing, c_recv.at[number]).wait()
        lax.fori_loop(0, DEPTHS - 1, sent(gathers[number]), 0)


def finish(out_v, gin_v, centre, sides, out_hbm, gin_hbm, gw_hbm, mixed, together, sem):
    out_copy = pltpu.make_async_copy(out_v, out_hbm, sem.at[0])
    gin_copy = pltpu.make_async_copy(gin_v, gin_hbm, sem.at[1])
    out_copy.start()
    gin_copy.start()
    for depth in range(DEPTHS):
        half = depth // 4
        for tap in range(3):
            for index, row in enumerate(ROW_ORDER):
                first = (3 * row + tap) * 4 + depth % 4
                start = 6 * tap + 3 * index - 3 if index else 3 * tap
                mixed[half, pl.ds(first, 3, stride=36)] = (sides if index else centre)[depth, start : start + 3]
    for half in range(2):
        together[:, :, half * 128 : (half + 1) * 128] = mixed[half].reshape(27, 4, 128)
    gw_copy = pltpu.make_async_copy(together, gw_hbm, sem.at[2])
    gw_copy.start()
    out_copy.wait()
    gin_copy.wait()
    gw_copy.wait()


def on_device(activations, weights, grad_output):
    vmem = pl.BlockSpec(memory_space=pltpu.VMEM)
    dma = pltpu.SemaphoreType.DMA
    hbm = pl.BlockSpec(memory_space=pltpu.HBM)
    results = pl.pallas_call(
        kernel,
        out_shape=(
            jax.ShapeDtypeStruct((2, 1, 64, 256), BF16),
            jax.ShapeDtypeStruct((2, 1, 64, 256), BF16),
            jax.ShapeDtypeStruct((DEPTHS, 9, 128), F32),
            jax.ShapeDtypeStruct((DEPTHS, 18, 128), F32),
        ),
        in_specs=[hbm] * 3,
        out_specs=(vmem,) * 4,
        scratch_shapes=[
            pltpu.VMEM((4, 3, 64, 256), BF16),
            pltpu.VMEM((4, 3, 64, 256), BF16),
            pltpu.VMEM((27, 256, 256), BF16),
            pltpu.VMEM((8, 32, 128), BF16),
            pltpu.VMEM((4, 8, 32, 128), BF16),
            pltpu.VMEM((2, 2, 4, 2, 64, 128), BF16),
            pltpu.VMEM((288, 2048), BF16),
            pltpu.VMEM((2048, 384), BF16),
            pltpu.VMEM((3, 288, 128), F32),
            pltpu.VMEM((LINES, 9, 128), F32),
            pltpu.VMEM((LINES, 18, 128), F32),
            pltpu.VMEM((LINES, 9, 128), F32),
            pltpu.VMEM((LINES, 18, 128), F32),
            pltpu.VMEM((9, 128), F32),
            pltpu.VMEM((18, 128), F32),
            pltpu.VMEM((2, 3, 128, 256), F32),
            dma((3,)),
            dma((32,)),
            dma((4,)),
            dma((8,)),
            dma((2,)),
            dma((2 * LINES,)),
            dma((2,)),
            dma((2 * DEPTHS,)),
            dma((2,)),
            dma((8,)),
            dma((8,)),
        ],
        compiler_params=pltpu.CompilerParams(
            collective_id=0, has_side_effects=True, vmem_limit_bytes=40 << 20
        ),
    )(*(pltpu.with_memory_space_constraint(operand, pltpu.HBM) for operand in (activations, weights, grad_output)))
    return pl.pallas_call(
        finish,
        out_shape=(
            jax.ShapeDtypeStruct((2, 1, 64, 256), BF16),
            jax.ShapeDtypeStruct((2, 1, 64, 256), BF16),
            jax.ShapeDtypeStruct((27, 4, 256), F32),
        ),
        in_specs=[vmem] * 4,
        out_specs=(hbm, hbm, hbm),
        scratch_shapes=[pltpu.VMEM((2, 108, 128), F32), pltpu.VMEM((27, 4, 256), F32), dma((3,))],
        compiler_params=pltpu.CompilerParams(vmem_limit_bytes=8 << 20),
    )(*results)


def solution(mesh):
    return jax.shard_map(
        on_device,
        mesh=mesh,
        in_specs=(P("sp", "chan", None, None), P(), P("sp", "chan", None, None)),
        out_specs=(P("sp", "chan", None, None), P("sp", "chan", None, None), P(None, "chan", None)),
        check_vma=False,
    )
```

```python
import functools

import jax
import jax.numpy as jnp
from jax import lax
from jax.experimental import pallas as pl
from jax.experimental.pallas import tpu as pltpu
from jax.sharding import PartitionSpec as P

MESH = pl.DeviceIdType.MESH
F32 = jnp.float32
BF16 = jnp.bfloat16

LINES = 32
DEPTHS = 8
ROW_ORDER = (1, 0, 2)


def shifted(value, by):
    width = value.shape[-2]
    rolled = pltpu.roll(value, by % width, value.ndim - 2)
    place = lax.broadcasted_iota(jnp.int32, value.shape, value.ndim - 2)
    return jnp.where(place == (0 if by == 1 else width - 1), 0.0, rolled)


def kernel(
    act_hbm, w_hbm, grad_hbm, out_ref, gin_ref, centre_out, sides_out,
    act_halo, grad_halo, w_v, act_t, act_all, grads, lhs, rhs, product, centre, sides, centre_in, sides_in, centre_sum, sides_sum, total,
    in_sem, act_send, act_recv, g_send, g_recv, b_send, b_recv, c_send, c_recv, halo_send, halo_recv,
):
    q, s = lax.axis_index("chan"), lax.axis_index("sp")
    m, l = q // 2, q % 2
    h, c = s // 2, s % 2

    z = 2 * h + l

    def at(line, side, depth):
        return (line * 2 + side, depth)

    def away(k, count):
        return count // 2 + jnp.where(k % 2 == 0, k // 2, -((k + 1) // 2))

    own_grad = pltpu.make_async_copy(grad_hbm.at[:, 0], grad_halo.at[pl.ds(1, 2), 1], in_sem.at[0])
    own_act = pltpu.make_async_copy(act_hbm.at[:, 0], act_halo.at[pl.ds(1, 2), 1], in_sem.at[1])
    own_w = pltpu.make_async_copy(w_hbm, w_v, in_sem.at[2])
    own_grad.start()
    own_act.start()
    own_w.start()

    has_outer = ((l == 0) & (m > 0)) | ((l == 1) & (m < LINES - 1))

    barrier = pltpu.get_barrier_semaphore()

    def greet(device):
        pl.semaphore_signal(barrier, inc=1, device_id=device, device_id_type=MESH)

    n = l * 8 + s

    def greet_line(k, carry):
        peer = (n + k) % 16
        greet(at(m, peer // 8, peer % 8))
        return carry

    lax.fori_loop(1, 16, greet_line, 0)

    @pl.when(has_outer)
    def _():
        greet(at(m - 1 + 2 * l, 1 - l, s))

    def greet_plane(k, carry):
        greet(at((m + k) % LINES, l, s))
        return carry

    lax.fori_loop(1, LINES, greet_plane, 0)

    for halo in (act_halo, grad_halo):
        @pl.when(q == 0)
        def _(halo=halo):
            halo[1:3, 0] = jnp.zeros((2, 64, 256), BF16)

        @pl.when(q == 2 * LINES - 1)
        def _(halo=halo):
            halo[1:3, 2] = jnp.zeros((2, 64, 256), BF16)

        @pl.when(s == 0)
        def _(halo=halo):
            halo[0] = jnp.zeros((3, 64, 256), BF16)

        @pl.when(s == DEPTHS - 1)
        def _(halo=halo):
            halo[3] = jnp.zeros((3, 64, 256), BF16)

    @pl.when(m == 0)
    def _():
        act_all[0] = jnp.zeros((8, 32, 128), BF16)

    @pl.when(m == LINES - 1)
    def _():
        act_all[3] = jnp.zeros((8, 32, 128), BF16)

    position = lax.broadcasted_iota(jnp.int32, (256, 256), 0)
    channel = lax.broadcasted_iota(jnp.int32, (256, 256), 1)
    select = jnp.where(channel == (position % 32) * 8 + position // 32, 1.0, 0.0).astype(BF16)
    own_act.wait()
    turned = lax.dot_general(
        select, act_halo[1:3, 1].reshape(128, 256), (((1,), (1,)), ((), ())), preferred_element_type=F32
    )
    act_t[...] = turned.astype(BF16).reshape(8, 32, 128)
    pl.semaphore_wait(barrier, 15 + LINES - 1 + jnp.where(has_outer, 1, 0))

    def halo_copy(halo, number, source, target, device):
        return functools.partial(
            pltpu.make_async_remote_copy,
            src_ref=source, dst_ref=target, send_sem=halo_send.at[number], recv_sem=halo_recv.at[number],
            device_id=device, device_id_type=MESH,
        )

    def row_copies(index, halo):
        for place, dq in enumerate((-1, 1)):
            source, target = halo.at[pl.ds(1, 2), 1], halo.at[pl.ds(1, 2), 1 - dq]
            copy = halo_copy(halo, 4 * index + place, source, target, (q + dq, s))
            yield (q + dq >= 0) & (q + dq < 2 * LINES), (q - dq >= 0) & (q - dq < 2 * LINES), copy

    def plane_copies(index, halo):
        for place, ds in enumerate((-1, 1)):
            source, target = halo.at[1 if ds == -1 else 2], halo.at[3 if ds == -1 else 0]
            copy = halo_copy(halo, 4 * index + 2 + place, source, target, (q, s + ds))
            yield (s + ds >= 0) & (s + ds < DEPTHS), (s - ds >= 0) & (s - ds < DEPTHS), copy

    both = ((0, act_halo), (1, grad_halo))

    def convolve(index, halo, planes):
        for tap in range(3):
            part = 0.0 if len(planes) == 1 else total[index, tap]
            for plane in planes:
                for row in range(3):
                    weight = w_v[(plane * 3 + row) * 3 + tap]
                    if index:
                        window, dims = halo[2 - plane : 4 - plane, 2 - row], (((1,), (1,)), ((), ()))
                    else:
                        window, dims = halo[plane : plane + 2, row], (((1,), (0,)), ((), ()))
                    part += lax.dot_general(window.reshape(128, 256), weight, dims, preferred_element_type=F32)
            total[index, tap] = part

    def joined(index):
        sums = [total[index, tap].reshape(2, 64, 256) for tap in range(3)]
        way = -1 if index else 1
        return (shifted(sums[0], way) + sums[1] + shifted(sums[2], -way)).astype(BF16)

    def grad_copy(k):
        there = (z + away(k, 8)) % 8
        half = pl.multiple_of(there // 4 * 128, 128)
        return pltpu.make_async_remote_copy(
            src_ref=grad_hbm.at[:, 0, :, pl.ds(half, 128)],
            dst_ref=grads.at[c, l, h],
            send_sem=g_send.at[k],
            recv_sem=g_recv.at[c],
            device_id=at(m, there % 2, there // 2 * 2 + c),
            device_id_type=MESH,
        )

    def in_line(k):
        there = (z + away(k // 2, 8)) % 8
        return there % 2, there // 2 * 2 + (c + 1 + k) % 2

    def act_copy(k):
        side, depth = in_line(k)
        return pltpu.make_async_remote_copy(
            src_ref=act_t.at[side * 4 + depth % 4],
            dst_ref=act_all.at[1 + l, s],
            send_sem=act_send.at[k],
            recv_sem=act_recv.at[1 + l],
            device_id=at(m, side, depth),
            device_id_type=MESH,
        )

    def outer_copy(row, way):
        return pltpu.make_async_remote_copy(
            src_ref=act_all.at[row],
            dst_ref=act_all.at[row - 2 * way],
            send_sem=act_send.at[15 + row],
            recv_sem=act_recv.at[row - 2 * way],
            device_id=at(m + way, l, s),
            device_id_type=MESH,
        )

    up, down = outer_copy(2, 1), outer_copy(1, -1)

    own_half = pl.multiple_of(h // 2 * 128, 128)
    grad_here = pltpu.make_async_copy(
        grad_hbm.at[:, 0, :, pl.ds(own_half, 128)], grads.at[c, l, h], g_recv.at[c]
    )
    act_here = pltpu.make_async_copy(act_t.at[l * 4 + s % 4], act_all.at[1 + l, s], act_recv.at[1 + l])
    grad_here.start()

    def start(copy):
        def step(k, carry):
            copy(k).start()
            return carry
        return step

    def sent(copy):
        def step(k, carry):
            copy(k).wait_send()
            return carry
        return step

    act_here.start()
    lax.fori_loop(0, 15, start(act_copy), 0)

    lax.fori_loop(0, 7, start(grad_copy), 0)

    def build_lhs(row, sides):
        here = act_all[row].astype(F32)
        turned = pltpu.roll(here, 64, 2)
        nothing = jnp.zeros((1, 32, 128), F32)
        low = lax.broadcasted_iota(jnp.int32, (8, 32, 128), 2) < 64
        down = jnp.where(low, jnp.concatenate([nothing, turned[:-1]]), turned).astype(BF16)
        up = jnp.where(low, turned, jnp.concatenate([turned[1:], nothing])).astype(BF16)
        for plane, value in enumerate((down, act_all[row], up)):
            for side in sides:
                first = (ROW_ORDER.index(row - side) * 3 + plane) * 32
                for depth in range(DEPTHS):
                    lane = depth % 2 * 1024 + side * 512 + depth // 2 * 128
                    lhs[first : first + 32, lane : lane + 128] = value[depth]

    def arrival(row):
        return pltpu.make_async_copy(act_all.at[row], act_all.at[row], act_recv.at[row])

    arrival(1).wait()
    pl.when(m > 0)(down.start)
    arrival(2).wait()
    pl.when(m < LINES - 1)(up.start)
    build_lhs(1, (0, 1))
    build_lhs(2, (0, 1))
    pltpu.make_async_copy(grads.at[c], grads.at[c], g_recv.at[c]).wait()
    pass_on = pltpu.make_async_remote_copy(
        src_ref=grads.at[c],
        dst_ref=grads.at[c],
        send_sem=g_send.at[7],
        recv_sem=g_recv.at[c],
        device_id=(q, s + 1 - 2 * c),
        device_id_type=MESH,
    )
    pass_on.start()
    own_grad.wait()
    for which in both:
        for there, _, copy in row_copies(*which):
            pl.when(there)(lambda copy=copy: copy().start())

    def build_rhs(core):
        for side in range(2):
            for depth in range(4):
                block = grads[core, side, depth].astype(F32)
                base = pl.multiple_of(core * 1024 + side * 512 + depth * 128, 128)
                for tap, moved in enumerate((shifted(block, -1), block, shifted(block, 1))):
                    rhs[pl.ds(base, 128), tap * 128 : (tap + 1) * 128] = moved.reshape(128, 128).astype(BF16)

    build_rhs(c)

    def multiply(rows, core, first):
        cells = pl.ds(pl.multiple_of(core * 1024, 1024), 1024)
        sums = jnp.dot(lhs[rows, cells], rhs[cells], preferred_element_type=F32)
        for tap in range(3):
            part = sums[:, tap * 128 : (tap + 1) * 128]
            product[tap, rows] = part if first else product[tap, rows] + part

    centre_rows, side_rows = slice(0, 96), slice(96, 288)
    multiply(centre_rows, c, True)
    pl.when(m > 0)(arrival(0).wait)
    build_lhs(0, (0,))
    pl.when(m < LINES - 1)(arrival(3).wait)
    build_lhs(3, (1,))
    multiply(side_rows, c, True)
    pltpu.make_async_copy(grads.at[1 - c], grads.at[1 - c], g_recv.at[1 - c]).wait()
    build_rhs(1 - c)

    def line_copy(buffer, landing, number):
        def copy(k):
            peer = (m // 8 + away(k % 4, 4)) % 4 * 8 + (m + away(k // 4, 8)) % 8
            return pltpu.make_async_remote_copy(
                src_ref=buffer.at[peer],
                dst_ref=landing.at[m],
                send_sem=b_send.at[number * LINES + k],
                recv_sem=b_recv.at[number],
                device_id=at(peer, l, s),
                device_id_type=MESH,
            )
        return copy

    centre_copy, sides_copy = line_copy(centre, centre_in, 0), line_copy(sides, sides_in, 1)


    multiply(centre_rows, 1 - c, False)
    for k in range(LINES):
        for tap in range(3):
            centre[k, 3 * tap : 3 * tap + 3] = product[tap, pl.ds(k, 3, stride=32)]
    pltpu.make_async_copy(centre.at[m], centre_in.at[m], b_recv.at[0]).start()
    lax.fori_loop(0, LINES - 1, start(centre_copy), 0)

    multiply(side_rows, 1 - c, False)
    for k in range(LINES):
        for tap in range(3):
            sides[k, 6 * tap : 6 * tap + 6] = product[tap, pl.ds(96 + k, 6, stride=32)]
    pltpu.make_async_copy(sides.at[m], sides_in.at[m], b_recv.at[1]).start()
    lax.fori_loop(0, LINES - 1, start(sides_copy), 0)

    own_w.wait()
    for which in both:
        for _, comes, copy in row_copies(*which):
            pl.when(comes)(lambda copy=copy: copy().wait_recv())
        for there, _, copy in plane_copies(*which):
            pl.when(there)(lambda copy=copy: copy().start())
    for which in both:
        convolve(*which, (1,))
    for _, comes, copy in plane_copies(*both[0]):
        pl.when(comes)(lambda copy=copy: copy().wait_recv())
    convolve(*both[0], (0, 2))
    out_ref[:, 0] = joined(0)

    def depth_copy(mine, landing, number):
        def copy(k):
            there = (h + away(k // 2, 4)) % 4
            return pltpu.make_async_remote_copy(
                src_ref=mine,
                dst_ref=landing.at[s],
                send_sem=c_send.at[number * DEPTHS + k],
                recv_sem=c_recv.at[number],
                device_id=(q, there * 2 + (c + 1 + k) % 2),
                device_id_type=MESH,
            )
        return copy

    gathers = []
    for number, (summands, mine, landing) in enumerate(
        ((centre_in, centre_sum, centre_out), (sides_in, sides_sum, sides_out))
    ):
        pltpu.make_async_copy(summands, summands, b_recv.at[number]).wait()
        mine[...] = sum(summands[k] for k in range(LINES)) * (1.0 / 256.0)
        pltpu.make_async_copy(mine, landing.at[s], c_recv.at[number]).start()
        gathers.append(depth_copy(mine, landing, number))
        lax.fori_loop(0, DEPTHS - 1, start(gathers[number]), 0)

    for _, comes, copy in plane_copies(*both[1]):
        pl.when(comes)(lambda copy=copy: copy().wait_recv())
    convolve(*both[1], (0, 2))
    gin_ref[:, 0] = joined(1)

    lax.fori_loop(0, 7, sent(grad_copy), 0)
    pass_on.wait_send()
    lax.fori_loop(0, 15, sent(act_copy), 0)

    pl.when(m < LINES - 1)(up.wait_send)
    pl.when(m > 0)(down.wait_send)

    for which in both:
        for copies in (row_copies, plane_copies):
            for there, _, copy in copies(*which):
                pl.when(there)(lambda copy=copy: copy().wait_send())
    lax.fori_loop(0, LINES - 1, sent(centre_copy), 0)
    lax.fori_loop(0, LINES - 1, sent(sides_copy), 0)

    for number, landing in enumerate((centre_out, sides_out)):
        pltpu.make_async_copy(landing, landing, c_recv.at[number]).wait()
        lax.fori_loop(0, DEPTHS - 1, sent(gathers[number]), 0)


def finish(out_v, gin_v, centre, sides, out_hbm, gin_hbm, gw_hbm, mixed, together, sem):
    out_copy = pltpu.make_async_copy(out_v, out_hbm, sem.at[0])
    gin_copy = pltpu.make_async_copy(gin_v, gin_hbm, sem.at[1])
    out_copy.start()
    gin_copy.start()
    for depth in range(DEPTHS):
        half = depth // 4
        for tap in range(3):
            for index, row in enumerate(ROW_ORDER):
                first = (3 * row + tap) * 4 + depth % 4
                start = 6 * tap + 3 * index - 3 if index else 3 * tap
                mixed[half, pl.ds(first, 3, stride=36)] = (sides if index else centre)[depth, start : start + 3]
    for half in range(2):
        together[:, :, half * 128 : (half + 1) * 128] = mixed[half].reshape(27, 4, 128)
    gw_copy = pltpu.make_async_copy(together, gw_hbm, sem.at[2])
    gw_copy.start()
    out_copy.wait()
    gin_copy.wait()
    gw_copy.wait()


def on_device(activations, weights, grad_output):
    vmem = pl.BlockSpec(memory_space=pltpu.VMEM)
    dma = pltpu.SemaphoreType.DMA
    hbm = pl.BlockSpec(memory_space=pltpu.HBM)
    results = pl.pallas_call(
        kernel,
        out_shape=(
            jax.ShapeDtypeStruct((2, 1, 64, 256), BF16),
            jax.ShapeDtypeStruct((2, 1, 64, 256), BF16),
            jax.ShapeDtypeStruct((DEPTHS, 9, 128), F32),
            jax.ShapeDtypeStruct((DEPTHS, 18, 128), F32),
        ),
        in_specs=[hbm] * 3,
        out_specs=(vmem,) * 4,
        scratch_shapes=[
            pltpu.VMEM((4, 3, 64, 256), BF16),
            pltpu.VMEM((4, 3, 64, 256), BF16),
            pltpu.VMEM((27, 256, 256), BF16),
            pltpu.VMEM((8, 32, 128), BF16),
            pltpu.VMEM((4, 8, 32, 128), BF16),
            pltpu.VMEM((2, 2, 4, 2, 64, 128), BF16),
            pltpu.VMEM((288, 2048), BF16),
            pltpu.VMEM((2048, 384), BF16),
            pltpu.VMEM((3, 288, 128), F32),
            pltpu.VMEM((LINES, 9, 128), F32),
            pltpu.VMEM((LINES, 18, 128), F32),
            pltpu.VMEM((LINES, 9, 128), F32),
            pltpu.VMEM((LINES, 18, 128), F32),
            pltpu.VMEM((9, 128), F32),
            pltpu.VMEM((18, 128), F32),
            pltpu.VMEM((2, 3, 128, 256), F32),
            dma((3,)),
            dma((32,)),
            dma((4,)),
            dma((8,)),
            dma((2,)),
            dma((2 * LINES,)),
            dma((2,)),
            dma((2 * DEPTHS,)),
            dma((2,)),
            dma((8,)),
            dma((8,)),
        ],
        compiler_params=pltpu.CompilerParams(
            collective_id=0, has_side_effects=True, vmem_limit_bytes=40 << 20
        ),
    )(*(pltpu.with_memory_space_constraint(operand, pltpu.HBM) for operand in (activations, weights, grad_output)))
    return pl.pallas_call(
        finish,
        out_shape=(
            jax.ShapeDtypeStruct((2, 1, 64, 256), BF16),
            jax.ShapeDtypeStruct((2, 1, 64, 256), BF16),
            jax.ShapeDtypeStruct((27, 4, 256), F32),
        ),
        in_specs=[vmem] * 4,
        out_specs=(hbm, hbm, hbm),
        scratch_shapes=[pltpu.VMEM((2, 108, 128), F32), pltpu.VMEM((27, 4, 256), F32), dma((3,))],
        compiler_params=pltpu.CompilerParams(vmem_limit_bytes=8 << 20),
    )(*results)


def solution(mesh):
    return jax.shard_map(
        on_device,
        mesh=mesh,
        in_specs=(P("sp", "chan", None, None), P(), P("sp", "chan", None, None)),
        out_specs=(P("sp", "chan", None, None), P("sp", "chan", None, None), P(None, "chan", None)),
        check_vma=False,
    )
```

```python
import functools

import jax
import jax.numpy as jnp
from jax import lax
from jax.experimental import pallas as pl
from jax.experimental.pallas import tpu as pltpu
from jax.sharding import PartitionSpec as P

MESH = pl.DeviceIdType.MESH
F32 = jnp.float32
BF16 = jnp.bfloat16

LINES = 32
DEPTHS = 8
ROW_ORDER = (1, 0, 2)


def shifted(value, by):
    width = value.shape[-2]
    rolled = pltpu.roll(value, by % width, value.ndim - 2)
    place = lax.broadcasted_iota(jnp.int32, value.shape, value.ndim - 2)
    return jnp.where(place == (0 if by == 1 else width - 1), 0.0, rolled)


def kernel(
    act_hbm, w_hbm, grad_hbm, out_ref, gin_ref, centre_out, sides_out,
    act_halo, grad_halo, w_v, act_t, act_all, grads, lhs, rhs, product, centre, sides, centre_in, sides_in, centre_sum, sides_sum, total,
    in_sem, act_send, act_recv, g_send, g_recv, b_send, b_recv, c_send, c_recv, halo_send, halo_recv,
):
    q, s = lax.axis_index("chan"), lax.axis_index("sp")
    m, l = q // 2, q % 2
    h, c = s // 2, s % 2

    z = 2 * h + l

    def at(line, side, depth):
        return (line * 2 + side, depth)

    def away(k, count):
        if isinstance(k, int):
            return count // 2 + (-((k + 1) // 2) if k % 2 else k // 2)
        return count // 2 + jnp.where(k % 2 == 0, k // 2, -((k + 1) // 2))

    own_grad = pltpu.make_async_copy(grad_hbm.at[:, 0], grad_halo.at[pl.ds(1, 2), 1], in_sem.at[0])
    own_act = pltpu.make_async_copy(act_hbm.at[:, 0], act_halo.at[pl.ds(1, 2), 1], in_sem.at[1])
    own_w = pltpu.make_async_copy(w_hbm, w_v, in_sem.at[2])
    own_grad.start()
    own_act.start()
    own_w.start()

    has_outer = ((l == 0) & (m > 0)) | ((l == 1) & (m < LINES - 1))

    barrier = pltpu.get_barrier_semaphore()

    def greet(device):
        pl.semaphore_signal(barrier, inc=1, device_id=device, device_id_type=MESH)

    n = l * 8 + s

    def greet_line(k, carry):
        peer = (n + k) % 16
        greet(at(m, peer // 8, peer % 8))
        return carry

    lax.fori_loop(1, 16, greet_line, 0)

    @pl.when(has_outer)
    def _():
        greet(at(m - 1 + 2 * l, 1 - l, s))

    def greet_plane(k, carry):
        greet(at((m + k) % LINES, l, s))
        return carry

    lax.fori_loop(1, LINES, greet_plane, 0)

    for halo in (act_halo, grad_halo):
        @pl.when(q == 0)
        def _(halo=halo):
            halo[1:3, 0] = jnp.zeros((2, 64, 256), BF16)

        @pl.when(q == 2 * LINES - 1)
        def _(halo=halo):
            halo[1:3, 2] = jnp.zeros((2, 64, 256), BF16)

        @pl.when(s == 0)
        def _(halo=halo):
            halo[0] = jnp.zeros((3, 64, 256), BF16)

        @pl.when(s == DEPTHS - 1)
        def _(halo=halo):
            halo[3] = jnp.zeros((3, 64, 256), BF16)

    @pl.when(m == 0)
    def _():
        act_all[0] = jnp.zeros((8, 32, 128), BF16)

    @pl.when(m == LINES - 1)
    def _():
        act_all[3] = jnp.zeros((8, 32, 128), BF16)

    position = lax.broadcasted_iota(jnp.int32, (256, 256), 0)
    channel = lax.broadcasted_iota(jnp.int32, (256, 256), 1)
    select = jnp.where(channel == (position % 32) * 8 + position // 32, 1.0, 0.0).astype(BF16)
    own_act.wait()
    turned = lax.dot_general(
        select, act_halo[1:3, 1].reshape(128, 256), (((1,), (1,)), ((), ())), preferred_element_type=F32
    )
    act_t[...] = turned.astype(BF16).reshape(8, 32, 128)
    pl.semaphore_wait(barrier, 15 + LINES - 1 + jnp.where(has_outer, 1, 0))

    def halo_copy(halo, number, source, target, device):
        return functools.partial(
            pltpu.make_async_remote_copy,
            src_ref=source, dst_ref=target, send_sem=halo_send.at[number], recv_sem=halo_recv.at[number],
            device_id=device, device_id_type=MESH,
        )

    def row_copies(index, halo):
        for place, dq in enumerate((-1, 1)):
            source, target = halo.at[pl.ds(1, 2), 1], halo.at[pl.ds(1, 2), 1 - dq]
            copy = halo_copy(halo, 4 * index + place, source, target, (q + dq, s))
            yield (q + dq >= 0) & (q + dq < 2 * LINES), (q - dq >= 0) & (q - dq < 2 * LINES), copy

    def plane_copies(index, halo):
        for place, ds in enumerate((-1, 1)):
            source, target = halo.at[1 if ds == -1 else 2], halo.at[3 if ds == -1 else 0]
            copy = halo_copy(halo, 4 * index + 2 + place, source, target, (q, s + ds))
            yield (s + ds >= 0) & (s + ds < DEPTHS), (s - ds >= 0) & (s - ds < DEPTHS), copy

    both = ((0, act_halo), (1, grad_halo))

    def convolve(index, halo, planes):
        for tap in range(3):
            part = 0.0 if len(planes) == 1 else total[index, tap]
            for plane in planes:
                for row in range(3):
                    weight = w_v[(plane * 3 + row) * 3 + tap]
                    if index:
                        window, dims = halo[2 - plane : 4 - plane, 2 - row], (((1,), (1,)), ((), ()))
                    else:
                        window, dims = halo[plane : plane + 2, row], (((1,), (0,)), ((), ()))
                    part += lax.dot_general(window.reshape(128, 256), weight, dims, preferred_element_type=F32)
            total[index, tap] = part

    def joined(index):
        sums = [total[index, tap].reshape(2, 64, 256) for tap in range(3)]
        way = -1 if index else 1
        return (shifted(sums[0], way) + sums[1] + shifted(sums[2], -way)).astype(BF16)

    def grad_copy(k):
        there = (z + away(k, 8)) % 8
        half = pl.multiple_of(there // 4 * 128, 128)
        return pltpu.make_async_remote_copy(
            src_ref=grad_hbm.at[:, 0, :, pl.ds(half, 128)],
            dst_ref=grads.at[c, l, h],
            send_sem=g_send.at[k],
            recv_sem=g_recv.at[c],
            device_id=at(m, there % 2, there // 2 * 2 + c),
            device_id_type=MESH,
        )

    def in_line(k):
        there = (z + away(k // 2, 8)) % 8
        return there % 2, there // 2 * 2 + (c + 1 + k) % 2

    def act_copy(k):
        side, depth = in_line(k)
        return pltpu.make_async_remote_copy(
            src_ref=act_t.at[side * 4 + depth % 4],
            dst_ref=act_all.at[1 + l, s],
            send_sem=act_send.at[k],
            recv_sem=act_recv.at[1 + l],
            device_id=at(m, side, depth),
            device_id_type=MESH,
        )

    def outer_copy(row, way):
        return pltpu.make_async_remote_copy(
            src_ref=act_all.at[row],
            dst_ref=act_all.at[row - 2 * way],
            send_sem=act_send.at[15 + row],
            recv_sem=act_recv.at[row - 2 * way],
            device_id=at(m + way, l, s),
            device_id_type=MESH,
        )

    up, down = outer_copy(2, 1), outer_copy(1, -1)

    own_half = pl.multiple_of(h // 2 * 128, 128)
    grad_here = pltpu.make_async_copy(
        grad_hbm.at[:, 0, :, pl.ds(own_half, 128)], grads.at[c, l, h], g_recv.at[c]
    )
    act_here = pltpu.make_async_copy(act_t.at[l * 4 + s % 4], act_all.at[1 + l, s], act_recv.at[1 + l])
    grad_here.start()

    def start(copy):
        def step(k, carry):
            copy(k).start()
            return carry
        return step

    def sent(copy):
        def step(k, carry):
            copy(k).wait_send()
            return carry
        return step

    act_here.start()
    for k in range(15):
        act_copy(k).start()

    for k in range(7):
        grad_copy(k).start()

    def build_lhs(row, sides):
        here = act_all[row].astype(F32)
        turned = pltpu.roll(here, 64, 2)
        nothing = jnp.zeros((1, 32, 128), F32)
        low = lax.broadcasted_iota(jnp.int32, (8, 32, 128), 2) < 64
        down = jnp.where(low, jnp.concatenate([nothing, turned[:-1]]), turned).astype(BF16)
        up = jnp.where(low, turned, jnp.concatenate([turned[1:], nothing])).astype(BF16)
        for plane, value in enumerate((down, act_all[row], up)):
            for side in sides:
                first = (ROW_ORDER.index(row - side) * 3 + plane) * 32
                for depth in range(DEPTHS):
                    lane = depth % 2 * 1024 + side * 512 + depth // 2 * 128
                    lhs[first : first + 32, lane : lane + 128] = value[depth]

    def arrival(row):
        return pltpu.make_async_copy(act_all.at[row], act_all.at[row], act_recv.at[row])

    arrival(1).wait()
    pl.when(m > 0)(down.start)
    arrival(2).wait()
    pl.when(m < LINES - 1)(up.start)
    build_lhs(1, (0, 1))
    build_lhs(2, (0, 1))
    pltpu.make_async_copy(grads.at[c], grads.at[c], g_recv.at[c]).wait()
    pass_on = pltpu.make_async_remote_copy(
        src_ref=grads.at[c],
        dst_ref=grads.at[c],
        send_sem=g_send.at[7],
        recv_sem=g_recv.at[c],
        device_id=(q, s + 1 - 2 * c),
        device_id_type=MESH,
    )
    pass_on.start()
    own_grad.wait()
    for which in both:
        for there, _, copy in row_copies(*which):
            pl.when(there)(lambda copy=copy: copy().start())

    def build_rhs(core):
        for side in range(2):
            for depth in range(4):
                block = grads[core, side, depth].astype(F32)
                base = pl.multiple_of(core * 1024 + side * 512 + depth * 128, 128)
                for tap, moved in enumerate((shifted(block, -1), block, shifted(block, 1))):
                    rhs[pl.ds(base, 128), tap * 128 : (tap + 1) * 128] = moved.reshape(128, 128).astype(BF16)

    build_rhs(c)

    def multiply(rows, core, first):
        cells = pl.ds(pl.multiple_of(core * 1024, 1024), 1024)
        sums = jnp.dot(lhs[rows, cells], rhs[cells], preferred_element_type=F32)
        for tap in range(3):
            part = sums[:, tap * 128 : (tap + 1) * 128]
            product[tap, rows] = part if first else product[tap, rows] + part

    centre_rows, side_rows = slice(0, 96), slice(96, 288)
    multiply(centre_rows, c, True)
    pl.when(m > 0)(arrival(0).wait)
    build_lhs(0, (0,))
    pl.when(m < LINES - 1)(arrival(3).wait)
    build_lhs(3, (1,))
    multiply(side_rows, c, True)
    pltpu.make_async_copy(grads.at[1 - c], grads.at[1 - c], g_recv.at[1 - c]).wait()
    build_rhs(1 - c)

    def line_copy(buffer, landing, number):
        def copy(k):
            peer = (m // 8 + away(k % 4, 4)) % 4 * 8 + (m + away(k // 4, 8)) % 8
            return pltpu.make_async_remote_copy(
                src_ref=buffer.at[peer],
                dst_ref=landing.at[m],
                send_sem=b_send.at[number * LINES + k],
                recv_sem=b_recv.at[number],
                device_id=at(peer, l, s),
                device_id_type=MESH,
            )
        return copy

    centre_copy, sides_copy = line_copy(centre, centre_in, 0), line_copy(sides, sides_in, 1)


    multiply(centre_rows, 1 - c, False)
    for k in range(LINES):
        for tap in range(3):
            centre[k, 3 * tap : 3 * tap + 3] = product[tap, pl.ds(k, 3, stride=32)]
    pltpu.make_async_copy(centre.at[m], centre_in.at[m], b_recv.at[0]).start()
    for k in range(LINES - 1):
        centre_copy(k).start()

    multiply(side_rows, 1 - c, False)
    for k in range(LINES):
        for tap in range(3):
            sides[k, 6 * tap : 6 * tap + 6] = product[tap, pl.ds(96 + k, 6, stride=32)]
    pltpu.make_async_copy(sides.at[m], sides_in.at[m], b_recv.at[1]).start()
    for k in range(LINES - 1):
        sides_copy(k).start()

    own_w.wait()
    for which in both:
        for _, comes, copy in row_copies(*which):
            pl.when(comes)(lambda copy=copy: copy().wait_recv())
        for there, _, copy in plane_copies(*which):
            pl.when(there)(lambda copy=copy: copy().start())
    for which in both:
        convolve(*which, (1,))
    for _, comes, copy in plane_copies(*both[0]):
        pl.when(comes)(lambda copy=copy: copy().wait_recv())
    convolve(*both[0], (0, 2))
    out_ref[:, 0] = joined(0)

    def depth_copy(mine, landing, number):
        def copy(k):
            there = (h + away(k // 2, 4)) % 4
            return pltpu.make_async_remote_copy(
                src_ref=mine,
                dst_ref=landing.at[s],
                send_sem=c_send.at[number * DEPTHS + k],
                recv_sem=c_recv.at[number],
                device_id=(q, there * 2 + (c + 1 + k) % 2),
                device_id_type=MESH,
            )
        return copy

    gathers = []
    for number, (summands, mine, landing) in enumerate(
        ((centre_in, centre_sum, centre_out), (sides_in, sides_sum, sides_out))
    ):
        pltpu.make_async_copy(summands, summands, b_recv.at[number]).wait()
        mine[...] = sum(summands[k] for k in range(LINES)) * (1.0 / 256.0)
        pltpu.make_async_copy(mine, landing.at[s], c_recv.at[number]).start()
        gathers.append(depth_copy(mine, landing, number))
        lax.fori_loop(0, DEPTHS - 1, start(gathers[number]), 0)

    for _, comes, copy in plane_copies(*both[1]):
        pl.when(comes)(lambda copy=copy: copy().wait_recv())
    convolve(*both[1], (0, 2))
    gin_ref[:, 0] = joined(1)

    lax.fori_loop(0, 7, sent(grad_copy), 0)
    pass_on.wait_send()
    lax.fori_loop(0, 15, sent(act_copy), 0)

    pl.when(m < LINES - 1)(up.wait_send)
    pl.when(m > 0)(down.wait_send)

    for which in both:
        for copies in (row_copies, plane_copies):
            for there, _, copy in copies(*which):
                pl.when(there)(lambda copy=copy: copy().wait_send())
    lax.fori_loop(0, LINES - 1, sent(centre_copy), 0)
    lax.fori_loop(0, LINES - 1, sent(sides_copy), 0)

    for number, landing in enumerate((centre_out, sides_out)):
        pltpu.make_async_copy(landing, landing, c_recv.at[number]).wait()
        lax.fori_loop(0, DEPTHS - 1, sent(gathers[number]), 0)


def finish(out_v, gin_v, centre, sides, out_hbm, gin_hbm, gw_hbm, mixed, together, sem):
    out_copy = pltpu.make_async_copy(out_v, out_hbm, sem.at[0])
    gin_copy = pltpu.make_async_copy(gin_v, gin_hbm, sem.at[1])
    out_copy.start()
    gin_copy.start()
    for depth in range(DEPTHS):
        half = depth // 4
        for tap in range(3):
            for index, row in enumerate(ROW_ORDER):
                first = (3 * row + tap) * 4 + depth % 4
                start = 6 * tap + 3 * index - 3 if index else 3 * tap
                mixed[half, pl.ds(first, 3, stride=36)] = (sides if index else centre)[depth, start : start + 3]
    for half in range(2):
        together[:, :, half * 128 : (half + 1) * 128] = mixed[half].reshape(27, 4, 128)
    gw_copy = pltpu.make_async_copy(together, gw_hbm, sem.at[2])
    gw_copy.start()
    out_copy.wait()
    gin_copy.wait()
    gw_copy.wait()


def on_device(activations, weights, grad_output):
    vmem = pl.BlockSpec(memory_space=pltpu.VMEM)
    dma = pltpu.SemaphoreType.DMA
    hbm = pl.BlockSpec(memory_space=pltpu.HBM)
    results = pl.pallas_call(
        kernel,
        out_shape=(
            jax.ShapeDtypeStruct((2, 1, 64, 256), BF16),
            jax.ShapeDtypeStruct((2, 1, 64, 256), BF16),
            jax.ShapeDtypeStruct((DEPTHS, 9, 128), F32),
            jax.ShapeDtypeStruct((DEPTHS, 18, 128), F32),
        ),
        in_specs=[hbm] * 3,
        out_specs=(vmem,) * 4,
        scratch_shapes=[
            pltpu.VMEM((4, 3, 64, 256), BF16),
            pltpu.VMEM((4, 3, 64, 256), BF16),
            pltpu.VMEM((27, 256, 256), BF16),
            pltpu.VMEM((8, 32, 128), BF16),
            pltpu.VMEM((4, 8, 32, 128), BF16),
            pltpu.VMEM((2, 2, 4, 2, 64, 128), BF16),
            pltpu.VMEM((288, 2048), BF16),
            pltpu.VMEM((2048, 384), BF16),
            pltpu.VMEM((3, 288, 128), F32),
            pltpu.VMEM((LINES, 9, 128), F32),
            pltpu.VMEM((LINES, 18, 128), F32),
            pltpu.VMEM((LINES, 9, 128), F32),
            pltpu.VMEM((LINES, 18, 128), F32),
            pltpu.VMEM((9, 128), F32),
            pltpu.VMEM((18, 128), F32),
            pltpu.VMEM((2, 3, 128, 256), F32),
            dma((3,)),
            dma((32,)),
            dma((4,)),
            dma((8,)),
            dma((2,)),
            dma((2 * LINES,)),
            dma((2,)),
            dma((2 * DEPTHS,)),
            dma((2,)),
            dma((8,)),
            dma((8,)),
        ],
        compiler_params=pltpu.CompilerParams(
            collective_id=0, has_side_effects=True, vmem_limit_bytes=40 << 20
        ),
    )(*(pltpu.with_memory_space_constraint(operand, pltpu.HBM) for operand in (activations, weights, grad_output)))
    return pl.pallas_call(
        finish,
        out_shape=(
            jax.ShapeDtypeStruct((2, 1, 64, 256), BF16),
            jax.ShapeDtypeStruct((2, 1, 64, 256), BF16),
            jax.ShapeDtypeStruct((27, 4, 256), F32),
        ),
        in_specs=[vmem] * 4,
        out_specs=(hbm, hbm, hbm),
        scratch_shapes=[pltpu.VMEM((2, 108, 128), F32), pltpu.VMEM((27, 4, 256), F32), dma((3,))],
        compiler_params=pltpu.CompilerParams(vmem_limit_bytes=8 << 20),
    )(*results)


def solution(mesh):
    return jax.shard_map(
        on_device,
        mesh=mesh,
        in_specs=(P("sp", "chan", None, None), P(), P("sp", "chan", None, None)),
        out_specs=(P("sp", "chan", None, None), P("sp", "chan", None, None), P(None, "chan", None)),
        check_vma=False,
    )
```
